128 devices in a mesh: section: 8 (over x, y_lo), attn: 16 (over y_hi, z, core).
Axes of the slice: x: 4, y: 4 (y_hi: 2, y_lo: 2; y = y_hi * 2 + y_lo), z: 4, core: 2. Of those that a mesh axis runs over, the one named last changes fastest.
Arguments:
- c_query: bfloat16 [64, 1536], P('section'), may hold values from -6 to 6
- up_query: bfloat16 [1536, 16384], P('section', 'attn'), may hold values from -0.15625 to 0.15625
- rope_query: bfloat16 [1536, 8192], P('section', 'attn'), may hold values from -0.15625 to 0.15625
- key_up: bfloat16 [512, 16384], P('section', 'attn'), may hold values from -0.5 to 0.5
- value_up: bfloat16 [512, 16384], P('section', 'attn'), may hold values from -0.5 to 0.5
- out_weight: bfloat16 [16384, 7168], P(None, ('section', 'attn')), may hold values from -0.09375 to 0.09375
- cache: bfloat16 [64, 8192, 576], P('section', 'attn'), may hold values from -340 to 340
- new_entry: bfloat16 [64, 576], P('section'), may hold values from -6 to 6
- lengths: int32 [64], P('section'), may hold values from 1024 to 8192, as said below
Outputs:
- mixed: bfloat16 [64, 7168], P('section', 'attn')
The draws below stay inside these ranges and needn't reach their ends.
Inputs may be any that keep to these rules, and one draw needn't show every extreme that they name: `lengths`: each row's count of filled slots; some row has all 8192 filled.
All inputs are finite; a program needn't handle non-finite values.
Results may differ from the reference program's by a relative error of at most 0.012.
The reference program's roundings to bfloat16 on the way count: a program that leaves them out, or rounds other values in their place, can miss the bound.
Values may be sent and summed in bfloat16 or wider, within the bound.
No kernel may reach another device: no remote copies, remote signals or barrier semaphores. Data moves between devices by JAX's collectives and lax.ppermute only.
A program may use at most 256 MiB of HBM per device.

```python
import jax
import jax.numpy as jnp
from jax import lax

D = 7168
HEADS = 128
QL = 1536
KL = 512
NOPE = 128
ROPE = 64
LEN = 8192
ROWS = 64
N_ATTN = 16


def draw_lengths(key, part):
    key = jax.random.fold_in(key, 11)
    key_vals, key_pick = jax.random.split(key)
    values = jax.random.randint(key_vals, (ROWS,), LEN // 8, LEN + 1)
    picked = jax.random.randint(key_pick, (), 0, ROWS)
    return jnp.where(jnp.arange(ROWS) == picked, LEN, values).astype(jnp.int32)


def draw_cache(key, part):
    key = jax.random.fold_in(key, 23)
    key_base = jax.random.fold_in(key, 0)
    shape_full = (ROWS, LEN, KL + ROPE)
    base_vals = jax.random.normal(key_base, shape_full, jnp.float32)
    return base_vals.astype(jnp.bfloat16)


def block_scale(stream_key, dims, pieces, low, largest):
    gain, own = 1.0, jax.random.fold_in(stream_key, 6)
    for axis_at, parts in pieces:
        draws = jnp.exp(jax.random.uniform(jax.random.fold_in(own, axis_at), (parts,), jnp.float32, low / len(pieces), largest / len(pieces)))
        gain = gain * jnp.repeat(draws, dims[axis_at] // parts).reshape([-1 if axis == axis_at else 1 for axis in range(len(dims))])
    return gain


def bell_draw(own_key, extent, width, reach, pieces=(), kind=jnp.bfloat16):
    drawn = jax.random.normal(own_key, extent, jnp.float32) * width
    if len(pieces) > 0:
        drawn = block_scale(own_key, extent, pieces, -0.22, 0.18) * drawn
    return jnp.clip(drawn, min=-reach, max=reach).astype(kind)


def setup_inputs(seed: int = 0) -> dict:
    streams_of = jax.random.split(jax.random.key(seed), 10)
    c_query = bell_draw(streams_of[0], (ROWS, QL), 1.0, 6.0, ((0, 8),))
    up_query = bell_draw(streams_of[1], (QL, HEADS * NOPE), QL ** -0.5, 0.15625, ((0, 8), (1, 16)))
    rope_query = bell_draw(streams_of[2], (QL, HEADS * ROPE), QL ** -0.5, 0.15625, ((0, 8), (1, 16)))
    key_up = bell_draw(streams_of[3], (KL, HEADS * NOPE), NOPE ** -0.5, 0.5, ((0, 8), (1, 16)))
    value_up = bell_draw(streams_of[4], (KL, HEADS * NOPE), NOPE ** -0.5, 0.5, ((0, 8), (1, 16)))
    out_weight = bell_draw(streams_of[5], (HEADS * NOPE, D), (HEADS * 32) ** -0.5, 0.09375, ((1, 128),))
    cache = draw_cache(jax.random.fold_in(streams_of[9], 71), 0)
    new_entry = bell_draw(streams_of[7], (ROWS, KL + ROPE), 1.0, 6.0, ((0, 8),))
    lengths = draw_lengths(jax.random.fold_in(streams_of[9], 71), 0)
    return dict(c_query=c_query, up_query=up_query, rope_query=rope_query, key_up=key_up, value_up=value_up, out_weight=out_weight, cache=cache, new_entry=new_entry, lengths=lengths)


def rotate_pairs(rope_part, position):
    half_width = rope_part.shape[-1] // 2
    freq_rates = 10000.0 ** (-jnp.arange(half_width, dtype=jnp.float32) / half_width)
    angles = position[..., None] * freq_rates
    cosine = jnp.cos(angles)
    sine_part = jnp.sin(angles)
    lower_half = rope_part[..., :half_width]
    upper_half = rope_part[..., half_width:]
    return jnp.concatenate([lower_half * cosine - upper_half * sine_part, lower_half * sine_part + upper_half * cosine], axis=-1)


def reference(c_query, up_query, rope_query, key_up, value_up, out_weight, cache, new_entry, lengths):
    score_scale = (NOPE + ROPE) ** -0.5
    position = lengths.astype(jnp.float32)

    def head_query(head):
        start_col = (head * NOPE).astype(jnp.int32)
        up_cols = lax.dynamic_slice_in_dim(up_query, start_col, NOPE, 1)
        key_cols = lax.dynamic_slice_in_dim(key_up, start_col, NOPE, 1)
        absorbed = jnp.dot(up_cols, key_cols.T, preferred_element_type=jnp.float32).astype(jnp.bfloat16)
        latent_part = jnp.dot(c_query, absorbed, preferred_element_type=jnp.float32)
        rope_cols = lax.dynamic_slice_in_dim(rope_query, (head * ROPE).astype(jnp.int32), ROPE, 1)
        rope_part = jnp.dot(c_query, rope_cols, preferred_element_type=jnp.float32)
        return jnp.concatenate([latent_part, rotate_pairs(rope_part, position)], axis=-1).astype(jnp.bfloat16)

    all_heads = lax.map(head_query, jnp.arange(HEADS, dtype=jnp.int32))
    queries = jnp.transpose(all_heads, (1, 0, 2))
    span = LEN // N_ATTN

    def one_row(inputs):
        row_query, row_cache, row_new, row_length = inputs
        scores = jnp.dot(row_query, row_cache.T, preferred_element_type=jnp.float32) * score_scale
        scores = scores.reshape(HEADS, N_ATTN, span)
        valid_mask = (jnp.arange(LEN, dtype=jnp.int32) < row_length).reshape(N_ATTN, span)
        masked = jnp.where(valid_mask[None], scores, -1e30)
        top_score = jnp.max(masked, axis=-1)
        probability = jnp.where(valid_mask[None], jnp.exp(masked - top_score[..., None]), 0.0)
        mass_sum = jnp.sum(probability, axis=-1)
        prob_low = lax.optimization_barrier(probability.astype(jnp.bfloat16))
        latent_cache = row_cache[:, :KL].reshape(N_ATTN, span, KL).astype(jnp.float32)
        weighted = jnp.einsum("hal,alc->hac", prob_low.astype(jnp.float32), latent_cache)
        partial_value = weighted / jnp.maximum(mass_sum, 1.0)[..., None]
        own_score = jnp.dot(row_query, row_new, preferred_element_type=jnp.float32) * score_scale
        highest = jnp.maximum(jnp.max(top_score, axis=-1), own_score)
        block_weight = mass_sum * jnp.exp(top_score - highest[:, None])
        new_weight = jnp.exp(own_score - highest)
        numer = jnp.sum(block_weight[..., None] * partial_value, axis=1) + new_weight[:, None] * row_new[:KL].astype(jnp.float32)[None, :]
        denom = jnp.sum(block_weight, axis=1) + new_weight
        return (numer / denom[:, None]).astype(jnp.bfloat16)

    latent_out = lax.map(one_row, (queries, cache, new_entry, lengths))

    def head_out(carry, head):
        start_col = (head * NOPE).astype(jnp.int32)
        value_cols = lax.dynamic_slice_in_dim(value_up, start_col, NOPE, 1)
        out_rows = lax.dynamic_slice_in_dim(out_weight, start_col, NOPE, 0)
        absorbed_out = jnp.dot(value_cols, out_rows, preferred_element_type=jnp.float32).astype(jnp.bfloat16)
        head_latent = lax.dynamic_index_in_dim(latent_out, head, 1, keepdims=False)
        return carry + jnp.dot(head_latent, absorbed_out, preferred_element_type=jnp.float32), None

    mixed, _ = lax.scan(head_out, jnp.zeros((ROWS, D), jnp.float32), jnp.arange(HEADS, dtype=jnp.int32))
    return mixed.astype(jnp.bfloat16)
```

```python
import functools

import jax
import jax.numpy as jnp
from jax import lax
from jax.experimental import pallas as pl
from jax.experimental.pallas import tpu as pltpu
from jax.sharding import Mesh
from jax.sharding import PartitionSpec as P

KL = 512
NOPE = 128
ROPE = 64
QDIM = KL + ROPE
HDEV = 8
RDEV = 8
PACK = KL + 128
SCALE = (NOPE + ROPE) ** -0.5
NEG = -1e30

ATTN = ("yh", "z", "core")
ALL = ("section",) + ATTN
bf16 = jnp.bfloat16
f32 = jnp.float32


def swap(x, axis, mask):
    names, size = (("section",), 8) if axis == "section" else (ATTN, 16)
    return lax.ppermute(x, names, [(i, i ^ mask) for i in range(size)])


def exchange(x, names):
    return lax.all_to_all(x, names, 0, 0, tiled=True)


def split3(x):
    a = x.astype(bf16).astype(f32)
    b = (x - a).astype(bf16).astype(f32)
    return a, b, x - a - b


def pack_stats(top, mass):
    terms = split3(top) + split3(mass)
    lane = lax.broadcasted_iota(jnp.int32, (top.shape[0], 128), 1)
    out = jnp.zeros((top.shape[0], 128), f32)
    for i, term in enumerate(terms):
        out = jnp.where(lane == i, term, out)
    return out


def unpack_stats(packed):
    top = packed[:, 0:1] + packed[:, 1:2] + packed[:, 2:3]
    mass = packed[:, 3:4] + packed[:, 4:5] + packed[:, 5:6]
    return top, mass


def query_kernel(order_ref, part_ref, key_ref, cos_ref, sin_ref, out_ref, key_scr, out_scr):
    q = part_ref[0]
    for i in range(1, 8):
        q = q + part_ref[i]
    for t in range(8):
        key_scr[t * 64:(t + 1) * 64, :] = key_ref[order_ref[t]]
    rope = q[:, HDEV * NOPE:]
    lane = lax.broadcasted_iota(jnp.int32, rope.shape, 1)
    up = pltpu.roll(rope, rope.shape[1] - ROPE // 2, 1)
    down = pltpu.roll(rope, ROPE // 2, 1)
    other = jnp.where(lane % ROPE < ROPE // 2, up, down)
    rope = rope * cos_ref[...] + other * sin_ref[...]
    for h in range(HDEV):
        qh = q[:, h * NOPE:(h + 1) * NOPE]
        hi = qh.astype(bf16)
        lo = (qh - hi.astype(f32)).astype(bf16)
        lhs = jnp.concatenate([hi.astype(f32), lo.astype(f32)], axis=0).astype(bf16)
        lat = lax.dot_general(
            lhs,
            key_scr[:, h * NOPE:(h + 1) * NOPE],
            (((1,), (1,)), ((), ())),
            preferred_element_type=f32,
        )
        lat = lat[0:8] + lat[8:16]
        tail = rope[:, h * ROPE:(h + 1) * ROPE]
        tail = jnp.concatenate([tail, jnp.zeros_like(tail)], axis=1)
        for j in range(4):
            out_scr[j, pl.ds(h, RDEV, stride=HDEV), :] = lat[:, j * 128:(j + 1) * 128]
        out_scr[4, pl.ds(h, RDEV, stride=HDEV), :] = tail
    for j in range(4):
        out_ref[:, j * 128:(j + 1) * 128] = out_scr[j].astype(bf16)
    out_ref[:, KL:QDIM] = out_scr[4, :, 0:ROPE].astype(bf16)


def make_queries(order, parts, key_blocks, cos, sin):
    vmem = pl.BlockSpec(memory_space=pltpu.VMEM)
    return pl.pallas_call(
        query_kernel,
        out_shape=jax.ShapeDtypeStruct((RDEV * HDEV, QDIM), bf16),
        in_specs=[pl.BlockSpec(memory_space=pltpu.SMEM)] + [vmem] * 4,
        out_specs=vmem,
        scratch_shapes=[
            pltpu.VMEM((KL, HDEV * NOPE), bf16),
            pltpu.VMEM((5, RDEV * HDEV, 128), f32),
        ],
        compiler_params=pltpu.CompilerParams(vmem_limit_bytes=24 * 1024 * 1024),
        name="make_queries",
    )(order, parts, key_blocks, cos, sin)


def attend_kernel(
    len_ref, at_ref, qa_ref, qb_ref, cache_ref, new_ref, keep_ref, send_ref, q_scr
):
    step = pl.program_id(0)

    @pl.when(step == 0)
    def _():
        q_scr[0:8] = qa_ref[...].astype(f32)
        q_scr[8:16] = qb_ref[...].astype(f32)

    first, owner = at_ref[0], at_ref[1]
    sends = []
    for i in range(2):
        row = step * 2 + i
        length = len_ref[row]
        at = pl.multiple_of(row * 8, 8)
        q = q_scr[:, pl.ds(at, 8), :].reshape(128, QDIM)
        keys = cache_ref[i]
        new = new_ref[i].astype(f32)
        own = jnp.sum(q * new, axis=1, keepdims=True) * SCALE
        score = (
            lax.dot_general(
                q.astype(bf16), keys, (((1,), (1,)), ((), ())), preferred_element_type=f32
            )
            * SCALE
        )
        slot = lax.broadcasted_iota(jnp.int32, score.shape, 1) + first
        valid = slot < length
        score = jnp.where(valid, score, NEG)
        top = jnp.max(score, axis=1, keepdims=True)
        prob = jnp.where(valid, jnp.exp(score - top), 0.0)
        mass = jnp.sum(prob, axis=1, keepdims=True)
        num = jnp.dot(prob.astype(bf16), keys[:, :KL], preferred_element_type=f32)
        mine = owner == 1
        own = jnp.where(mine, own, NEG)
        best = jnp.maximum(top, own)
        scale_old = jnp.exp(top - best)
        scale_new = jnp.where(mine, jnp.exp(own - best), 0.0)
        num = num * scale_old + scale_new * new[:, :KL]
        mass = mass * scale_old + scale_new
        stats = pack_stats(best, mass)
        keep_ref[:, pl.ds(at, 8), 0:KL] = num[0:64].reshape(8, 8, KL)
        keep_ref[:, pl.ds(at, 8), KL:PACK] = stats[0:64].reshape(8, 8, 128)
        sends.append(
            jnp.concatenate([num[64:128], stats[64:128]], axis=1).reshape(8, 8, PACK)
        )
    at = pl.multiple_of(step * 16, 16)
    send_ref[:, pl.ds(at, 16), :] = jnp.concatenate(sends, axis=1).astype(bf16)


def attend(lengths, place, qa, qb, cache, new):
    full = lambda *shape: pl.BlockSpec(shape, lambda r, *_: (0,) * len(shape))
    grid_spec = pltpu.PrefetchScalarGridSpec(
        num_scalar_prefetch=2,
        grid=(RDEV // 2,),
        in_specs=[
            full(8, 64, QDIM),
            full(8, 64, QDIM),
            pl.BlockSpec((2, cache.shape[1], QDIM), lambda r, *_: (r, 0, 0)),
            pl.BlockSpec((2, 1, QDIM), lambda r, *_: (r, 0, 0)),
        ],
        out_specs=[full(8, 64, PACK), full(8, 64, PACK)],
        scratch_shapes=[pltpu.VMEM((16, 64, QDIM), f32)],
    )
    return pl.pallas_call(
        attend_kernel,
        grid_spec=grid_spec,
        out_shape=[
            jax.ShapeDtypeStruct((8, 64, PACK), f32),
            jax.ShapeDtypeStruct((8, 64, PACK), bf16),
        ],
        compiler_params=pltpu.CompilerParams(vmem_limit_bytes=40 * 1024 * 1024),
        name="attend",
    )(lengths, place, qa, qb, cache, new)


def merge_kernel(keep_ref, got_ref, out_ref):
    for i in range(8):
        mine = keep_ref[i]
        other = got_ref[i].astype(f32)
        top_a, mass_a = unpack_stats(mine[:, KL:])
        top_b, mass_b = unpack_stats(other[:, KL:])
        best = jnp.maximum(top_a, top_b)
        wa, wb = jnp.exp(top_a - best), jnp.exp(top_b - best)
        num = mine[:, :KL] * wa + other[:, :KL] * wb
        out_ref[i, :, 0:KL] = num.astype(bf16)
        out_ref[i, :, KL:PACK] = pack_stats(best, mass_a * wa + mass_b * wb).astype(bf16)


def merge(keep, got):
    vmem = pl.BlockSpec(memory_space=pltpu.VMEM)
    return pl.pallas_call(
        merge_kernel,
        out_shape=jax.ShapeDtypeStruct((8, 64, PACK), bf16),
        in_specs=[vmem, vmem],
        out_specs=vmem,
        compiler_params=pltpu.CompilerParams(vmem_limit_bytes=24 * 1024 * 1024),
        name="merge",
    )(keep, got)


def combine_kernel(got_ref, value_ref, out_ref, lat_scr):
    tops, masses = [], []
    for i in range(8):
        top, mass = unpack_stats(got_ref[i, :, KL:PACK].astype(f32))
        tops.append(top)
        masses.append(mass)
    best = functools.reduce(jnp.maximum, tops)
    num = jnp.zeros((64, KL), f32)
    den = jnp.zeros((64, 1), f32)
    for i in range(8):
        w = jnp.exp(tops[i] - best)
        num = num + got_ref[i, :, 0:KL].astype(f32) * w
        den = den + masses[i] * w
    lat = num / den
    for j in range(4):
        lat_scr[j] = lat[:, j * 128:(j + 1) * 128]
    for h in range(HDEV):
        lat = jnp.concatenate(
            [lat_scr[j, pl.ds(h, RDEV, stride=HDEV), :] for j in range(4)], axis=1
        ).astype(bf16)
        out_ref[:, h * NOPE:(h + 1) * NOPE] = jnp.dot(
            lat, value_ref[:, h * NOPE:(h + 1) * NOPE], preferred_element_type=f32
        )


def combine(got, value):
    vmem = pl.BlockSpec(memory_space=pltpu.VMEM)
    return pl.pallas_call(
        combine_kernel,
        out_shape=jax.ShapeDtypeStruct((RDEV, HDEV * NOPE), f32),
        in_specs=[vmem, vmem],
        out_specs=vmem,
        scratch_shapes=[pltpu.VMEM((4, 64, 128), f32)],
        compiler_params=pltpu.CompilerParams(vmem_limit_bytes=24 * 1024 * 1024),
        name="combine",
    )(got, value)


def rotary_tables(lengths):
    half = ROPE // 2
    rates = 10000.0 ** (-jnp.arange(half, dtype=f32) / half)
    angles = lengths.astype(f32)[:, None] * rates
    cosine, sine = jnp.cos(angles), jnp.sin(angles)
    cos = jnp.tile(jnp.concatenate([cosine, cosine], axis=1), (1, HDEV))
    sin = jnp.tile(jnp.concatenate([-sine, sine], axis=1), (1, HDEV))
    return cos, sin


def canonical(blocks, axis, index):
    for bit in range(len(blocks).bit_length() - 1):
        flip = (index >> bit) & 1 == 1
        blocks = [jnp.where(flip, blocks[j ^ (1 << bit)], blocks[j]) for j in range(len(blocks))]
    return jnp.stack(blocks, axis=axis)


def swapped_out_weight(out_weight, core, z):
    cols = out_weight.shape[1]
    rows = out_weight.T.reshape(cols, 2, 4, 2, HDEV * NOPE)
    keep = lax.dynamic_index_in_dim(rows, core, 3, keepdims=False)
    send = lax.dynamic_index_in_dim(rows, 1 - core, 3, keepdims=False)
    pair = jnp.stack([keep, swap(send, "attn", 1)])
    out = [None] * 4
    out[0] = lax.dynamic_index_in_dim(pair, z, 3, keepdims=False)
    for j, mask in ((1, 2), (3, 6), (2, 4)):
        out[j] = swap(lax.dynamic_index_in_dim(pair, z ^ j, 3, keepdims=False), "attn", mask)
    return out


def on_device(
    c_query, up_query, rope_query, key_up, value_up, out_weight, cache, new_entry, lengths
):
    section = lax.axis_index("section")
    yh, z, core = (lax.axis_index(n) for n in ATTN)
    attn = yh * 8 + z * 2 + core
    span = cache.shape[1]

    with jax.named_scope("weights"):
        keys = [key_up]
        for mask in (1, 2, 6):
            keys = keys + [None] * len(keys)
            half = len(keys) // 2
            got = swap(jnp.stack(keys[:half]), "section", mask)
            for j in range(half):
                keys[half + j] = got[j]
        offsets = [0, 1, 2, 3, 6, 7, 4, 5]
        place_of = jnp.array([offsets.index(j) for j in range(8)], jnp.int32)
        order = place_of[section ^ jnp.arange(8, dtype=jnp.int32)]
        key_blocks = jnp.stack(keys)
        value = lax.all_gather(value_up, "section", axis=0, tiled=True)
        weight = swapped_out_weight(out_weight, core, z)
        cos, sin = rotary_tables(lengths)
        up = jnp.concatenate([up_query, rope_query], axis=1)

    with jax.named_scope("queries"):
        rows = exchange(
            jnp.transpose(c_query.reshape(RDEV, 8, -1), (1, 0, 2)), ("section",)
        ).reshape(64, -1)
        part = jnp.dot(rows, up, preferred_element_type=f32).reshape(8, RDEV, -1)
        parts = exchange(part, ("section",))
        queries = make_queries(order, parts, key_blocks, cos, sin)
        qa = exchange(jnp.broadcast_to(queries[None], (8,) + queries.shape), ("yh", "z"))
        qb = swap(qa, "attn", 1)

    with jax.named_scope("attention"):
        place = jnp.stack([attn * span, (attn == 0).astype(jnp.int32)])
        keep, send = attend(lengths, place, qa, qb, cache, new_entry[:, None, :].astype(f32))
        merged = merge(keep, swap(send, "attn", 1))
        got = exchange(merged, ("yh", "z"))

    with jax.named_scope("output"):
        mid = combine(got, value).astype(bf16)
        mids = exchange(jnp.broadcast_to(mid[None], (16,) + mid.shape), ("section", "yh"))
        mids = jnp.transpose(mids.reshape(8, 2, RDEV, -1), (0, 2, 1, 3)).reshape(64, 2, -1)
        outs = [
            lax.dot_general(
                mids, w, (((1, 2), (2, 3)), ((), ())), preferred_element_type=f32
            )
            for w in weight
        ]
        outs = [jnp.stack([o[:, 0], o[:, 1]], 1) for o in outs]
        outs = canonical(outs, 1, z)
        outs = canonical([outs[:, :, 0], outs[:, :, 1]], 2, core)
        share = exchange(outs.reshape(8, RDEV, -1), ("z", "core"))
        mixed = jnp.sum(share, axis=0).astype(bf16)
        return lax.ppermute(
            mixed,
            ALL,
            [
                (s * 16 + y * 8 + t, t * 16 + s * 2 + y)
                for s in range(8)
                for y in range(2)
                for t in range(8)
            ],
        )


def solution(mesh):
    split = Mesh(mesh.devices.reshape(8, 2, 4, 2), ALL)
    return jax.shard_map(
        on_device,
        mesh=split,
        in_specs=(
            P("section", None),
            P("section", ATTN),
            P("section", ATTN),
            P("section", ATTN),
            P("section", ATTN),
            P(None, ALL),
            P("section", ATTN, None),
            P("section", None),
            P("section"),
        ),
        out_specs=P("section", ATTN),
        check_vma=False,
    )
```

```python
import functools

import jax
import jax.numpy as jnp
from jax import lax
from jax.experimental import pallas as pl
from jax.experimental.pallas import tpu as pltpu
from jax.sharding import Mesh
from jax.sharding import PartitionSpec as P

KL = 512
NOPE = 128
ROPE = 64
QDIM = KL + ROPE
SLICE = 192
PACK = KL + 128
ROWS = 64
SCALE = (NOPE + ROPE) ** -0.5
NEG = -1e30

ATTN = ("yh", "z", "core")
ALL = ("section",) + ATTN
bf16 = jnp.bfloat16
f32 = jnp.float32

VMEM = pl.BlockSpec(memory_space=pltpu.VMEM)
SMEM = pl.BlockSpec(memory_space=pltpu.SMEM)
ANY = pl.BlockSpec(memory_space=pl.ANY)
HBM = pl.BlockSpec(memory_space=pltpu.HBM)
NT = (((1,), (1,)), ((), ()))


def swap(x, mask):
    return lax.ppermute(x, ATTN, [(i, i ^ mask) for i in range(16)])


def exchange(x, names):
    return lax.all_to_all(x, names, 0, 0, tiled=True)


def call(kernel, out_shape, in_specs, args, scratch=(), out_specs=None, limit=32):
    if out_specs is None:
        out_specs = jax.tree.map(lambda _: VMEM, out_shape)
    return pl.pallas_call(
        kernel,
        out_shape=out_shape,
        in_specs=in_specs,
        out_specs=out_specs,
        scratch_shapes=list(scratch),
        compiler_params=pltpu.CompilerParams(vmem_limit_bytes=limit * 1024 * 1024),
        name=kernel.__name__,
    )(*args)


def shaped(dtype, *shape):
    return jax.ShapeDtypeStruct(shape, dtype)


def pack_stats(top, mass):
    lane = lax.broadcasted_iota(jnp.int32, top.shape, 1)
    out = jnp.zeros(top.shape, f32)
    for start, value in ((0, top), (3, mass)):
        for i in range(3):
            term = value.astype(bf16).astype(f32)
            out = jnp.where(lane == start + i, term, out)
            value = value - term
    return out


def unpack_stats(packed):
    row = lax.broadcasted_iota(jnp.int32, (128, 256), 0)
    col = lax.broadcasted_iota(jnp.int32, (128, 256), 1)
    low = jnp.where(col < 128, 0, 3)
    pick = jnp.where((row >= low) & (row < low + 3), 1.0, 0.0).astype(bf16)
    both = jnp.dot(packed, pick, preferred_element_type=f32)
    return both[:, :128], both[:, 128:]


def widen(x):
    return jnp.concatenate([x] * (KL // 128), axis=1)


def blocks_kernel(at_ref, weight_ref, *refs):
    outs, sems = refs[:4], refs[4]
    copies = []
    for j in range(4):
        for c in range(2):
            for y in range(2):
                start = pl.multiple_of((y * 8 + (at_ref[0] ^ j) * 2 + c) * 1024, 1024)
                copies.append(
                    pltpu.make_async_copy(
                        weight_ref.at[:, pl.ds(start, 1024)],
                        outs[j].at[c, y],
                        sems.at[j * 4 + c * 2 + y],
                    )
                )
    for copy in copies:
        copy.start()
    for copy in copies:
        copy.wait()


def pick_kernel(at_ref, *refs):
    pieces, out_ref, sems = refs[:4], refs[4], refs[5]
    copies = [
        pltpu.make_async_copy(pieces[j].at[1 - at_ref[1]], out_ref.at[j], sems.at[j])
        for j in range(4)
    ]
    for copy in copies:
        copy.start()
    for copy in copies:
        copy.wait()


def slices_kernel(length_ref, query_ref, key_ref, value_ref, early_ref, out_ref, query_scr, sems):
    copies = [pltpu.make_async_copy(query_ref, query_scr, sems.at[16])]
    for j in range(8):
        cols = pl.ds(j * 128, 128)
        for i, ref in enumerate((key_ref, value_ref)):
            copies.append(
                pltpu.make_async_copy(
                    ref.at[:, cols], out_ref.at[j, pl.ds(i * 64, 64), :], sems.at[j * 2 + i]
                )
            )
    for copy in copies:
        copy.start()
    lane = lax.broadcasted_iota(jnp.int32, (8, ROPE), 1)
    row = lax.broadcasted_iota(jnp.int32, (8, ROPE), 0)
    length = jnp.zeros((8, ROPE), jnp.int32)
    for r in range(8):
        length = jnp.where(row == r, length_ref[r], length)
    length = length.astype(f32)
    high = length.astype(bf16).astype(f32)
    tail = jnp.where(lane == 0, high, jnp.where(lane == 1, length - high, 0.0))
    copies[0].wait()
    query = query_scr[...].astype(f32)
    for j in range(8):
        piece = query[:, j * SLICE:(j + 1) * SLICE]
        rest = jnp.concatenate([piece[:, 128:], tail], axis=1)
        out_ref[j, 128:144, :] = jnp.concatenate([piece[:, :128], rest], axis=0).astype(bf16)
    for copy in copies[1:]:
        copy.wait()


def partial_kernel(got_ref, up_hbm, rope_hbm, out_ref, up_ref, rope_ref, sems):
    copies = [
        pltpu.make_async_copy(up_hbm, up_ref, sems.at[0]),
        pltpu.make_async_copy(rope_hbm, rope_ref, sems.at[1]),
    ]
    for copy in copies:
        copy.start()
    tiles = [got_ref[t, 128:144, :].astype(f32) for t in range(8)]
    rows = jnp.concatenate(
        [
            jnp.concatenate([x[0:8] for x in tiles], axis=0),
            jnp.concatenate([x[8:16] for x in tiles], axis=0)[:, :ROPE],
        ],
        axis=1,
    ).astype(bf16)
    for copy in copies:
        copy.wait()
    nope = jnp.dot(rows, up_ref[...], preferred_element_type=f32)
    rope = jnp.dot(rows, rope_ref[...], preferred_element_type=f32)
    for h in range(8):
        out_ref[h, :, 0:NOPE] = nope[:, h * NOPE:(h + 1) * NOPE]
        out_ref[h, :, NOPE:SLICE] = rope[:, h * ROPE:(h + 1) * ROPE]


def query_kernel(part_ref, got_ref, cos_ref, sin_ref, *refs):
    out_ref = refs[-1]
    q = part_ref[0]
    for i in range(1, 8):
        q = q + part_ref[i]
    nope = q[:, :NOPE]
    high = nope.astype(bf16).astype(f32)
    lhs = jnp.concatenate([high, nope - high], axis=0).astype(bf16)
    key = jnp.concatenate([got_ref[t, 0:64, :] for t in range(8)], axis=0)
    lat = lax.dot_general(lhs, key, NT, preferred_element_type=f32)
    lat = lat[:ROWS] + lat[ROWS:]
    a, b = q[:, NOPE:NOPE + ROPE // 2], q[:, NOPE + ROPE // 2:]
    cos, sin = cos_ref[...], sin_ref[...]
    rope = jnp.concatenate([a * cos - b * sin, a * sin + b * cos], axis=1)
    for s in range(8):
        at = slice(s * 8, s * 8 + 8)
        out_ref[s, :, 0:KL] = jnp.concatenate([lat[at]] * 8, axis=0).astype(bf16)
        out_ref[s, :, KL:QDIM] = jnp.concatenate([rope[at]] * 8, axis=0).astype(bf16)


def attend_kernel(len_ref, at_ref, qa_ref, qb_ref, cache_ref, new_ref, *refs):
    keep_ref, send_ref, q_scr, send_scr, cache_scr, sems = refs[-6:]
    copies = [
        pltpu.make_async_copy(cache_ref.at[r], cache_scr.at[r], sems.at[r]) for r in range(8)
    ]
    for copy in copies:
        copy.start()
    for j in range(5):
        width = min(128, QDIM - j * 128)
        at = slice(j * 128, j * 128 + width)
        q_scr[j, 0:512, 0:width] = qa_ref[:, at].astype(f32)
        q_scr[j, 512:1024, 0:width] = qb_ref[:, at].astype(f32)
    first, mine = at_ref[0], at_ref[1] == 1
    news = new_ref[...].astype(f32)
    for r in range(8):
        heads = pl.ds(r, 128, stride=8)
        q = jnp.concatenate(
            [q_scr[j, heads, :] for j in range(4)] + [q_scr[4, heads, :][:, :ROPE]], axis=1
        )
        new = news[r:r + 1, :]
        own = jnp.sum(q * new, axis=1, keepdims=True) * SCALE
        copies[r].wait()
        score = jnp.dot(q.astype(bf16), cache_scr[r], preferred_element_type=f32) * SCALE
        slot = lax.broadcasted_iota(jnp.int32, score.shape, 1) + first
        valid = slot < len_ref[r]
        score = jnp.where(valid, score, NEG)
        top = jnp.max(score, axis=1, keepdims=True)
        prob = jnp.where(valid, jnp.exp(score - top), 0.0)
        mass = jnp.sum(prob, axis=1, keepdims=True)
        num = lax.dot_general(
            prob.astype(bf16), cache_scr[r, 0:KL, :], NT, preferred_element_type=f32
        )
        own = jnp.where(mine, own, NEG)
        best = jnp.maximum(top, own)
        scale_old = jnp.exp(top - best)
        scale_new = jnp.where(mine, jnp.exp(own - best), 0.0)
        num = num * scale_old + scale_new * new[:, :KL]
        mass = mass * scale_old + scale_new
        stats = pack_stats(
            jnp.broadcast_to(best, (128, 128)), jnp.broadcast_to(mass, (128, 128))
        )
        half = pl.ds(r, 64, stride=8)
        for j in range(5):
            tile = num[:, j * 128:(j + 1) * 128] if j < 4 else stats
            keep_ref[j, half, :] = tile[0:64]
            send_scr[j, half, :] = tile[64:128]
    for j in range(5):
        send_ref[:, j * 128:(j + 1) * 128] = send_scr[j].astype(bf16)


def merge_kernel(keep_ref, got_ref, out_ref):
    for i in range(8):
        at = slice(i * 64, i * 64 + 64)
        top_a, mass_a = unpack_stats(keep_ref[4, at, :].astype(bf16))
        top_b, mass_b = unpack_stats(got_ref[at, KL:PACK])
        best = jnp.maximum(top_a, top_b)
        wa, wb = jnp.exp(top_a - best), jnp.exp(top_b - best)
        for j in range(4):
            cols = slice(j * 128, j * 128 + 128)
            num = keep_ref[j, at, :] * wa + got_ref[at, cols].astype(f32) * wb
            out_ref[at, cols] = num.astype(bf16)
        out_ref[at, KL:PACK] = pack_stats(best, mass_a * wa + mass_b * wb).astype(bf16)


def combine_kernel(got_ref, first_ref, out_ref):
    value = jnp.concatenate([first_ref[t, 64:128, :] for t in range(8)], axis=0)
    latents = []
    for s in range(8):
        top, mass = unpack_stats(got_ref[s, :, KL:PACK])
        top = top.reshape(8, 8, 128)
        best = jnp.max(top, axis=0)
        w = jnp.exp(top - best[None])
        den = jnp.sum(mass.reshape(8, 8, 128) * w, axis=0)
        num = [
            jnp.sum(
                got_ref[s, :, j * 128:(j + 1) * 128].astype(f32).reshape(8, 8, 128) * w, axis=0
            )
            / den
            for j in range(4)
        ]
        latents.append(jnp.concatenate(num, axis=1))
    latent = jnp.concatenate(latents, axis=0).astype(bf16)
    mid = jnp.dot(latent, value, preferred_element_type=f32).astype(bf16)
    for i in range(16):
        out_ref[i] = mid


def project_kernel(at_ref, mid_ref, *refs):
    pieces, other_ref, out_ref = refs[:4], refs[4], refs[5]
    lhs = [
        jnp.concatenate([mid_ref[i * 2 + y] for i in range(8)], axis=1) for y in range(2)
    ]
    for j in range(4):
        tile = []
        for k in range(2):
            out = sum(
                lax.dot_general(
                    lhs[y],
                    other_ref[j, y] if k else pieces[j][at_ref[1], y],
                    NT,
                    preferred_element_type=f32,
                )
                for y in range(2)
            )
            tile += [out, jnp.zeros((ROWS, 8), f32)]
        out_ref[:, j * 128:(j + 1) * 128] = jnp.concatenate(tile, axis=1)


def total_kernel(share_ref, out_ref):
    total = [jnp.zeros((8, 128), f32) for _ in range(4)]
    for t in range(8):
        for k in range(4):
            tile = share_ref[t, :, (k ^ (t >> 1)) * 128:((k ^ (t >> 1)) + 1) * 128]
            if t & 1:
                tile = jnp.concatenate([tile[:, 64:], tile[:, :64]], axis=1)
            total[k] = total[k] + tile
    out_ref[...] = jnp.concatenate(
        [total[k // 2][:, (k % 2) * 64:(k % 2) * 64 + 56] for k in range(8)], axis=1
    ).astype(bf16)


def on_device(
    c_query, up_query, rope_query, key_up, value_up, out_weight, cache, new_entry, lengths
):
    yh, z, core = (lax.axis_index(n) for n in ATTN)
    attn = yh * 8 + z * 2 + core
    where = jnp.stack([z, core])
    span = cache.shape[1]

    with jax.named_scope("weights"):
        pieces = call(
            blocks_kernel,
            [shaped(bf16, 2, 2, 56, 1024)] * 4,
            [SMEM, HBM],
            (where, out_weight.T),
            [pltpu.SemaphoreType.DMA((16,))],
        )
        pieces = [p if j == 0 else swap(p, j * 2) for j, p in enumerate(pieces)]
        others = swap(
            call(
                pick_kernel,
                shaped(bf16, 4, 2, 56, 1024),
                [SMEM] + [ANY] * 4,
                (where, *pieces),
                [pltpu.SemaphoreType.DMA((4,))],
            ),
            1,
        )

    with jax.named_scope("queries"):
        slices = call(
            slices_kernel,
            shaped(bf16, 8, 144, 128),
            [SMEM] + [HBM] * 3 + [ANY],
            (lengths, c_query, key_up, value_up, pieces[0]),
            [pltpu.VMEM(c_query.shape, bf16), pltpu.SemaphoreType.DMA((17,))],
        )
        first = exchange(slices, ("section",))
        part = call(
            partial_kernel,
            shaped(f32, 8, ROWS, SLICE),
            [VMEM, HBM, HBM],
            (first, up_query, rope_query),
            [
                pltpu.VMEM(up_query.shape, bf16),
                pltpu.VMEM(rope_query.shape, bf16),
                pltpu.SemaphoreType.DMA((2,)),
            ],
        )
        parts = exchange(part, ("section",))
        position = (
            first[:, 136:144, ROPE].astype(f32) + first[:, 136:144, ROPE + 1].astype(f32)
        ).reshape(ROWS)
        half = ROPE // 2
        rates = 10000.0 ** (-jnp.arange(half, dtype=f32) / half)
        angles = position[:, None] * rates
        queries = call(
            query_kernel,
            shaped(bf16, 8, 64, QDIM),
            [VMEM] * 4 + [ANY] * 3,
            (parts, first, jnp.cos(angles), jnp.sin(angles), pieces[1], pieces[2], pieces[3]),
        )
        qa = exchange(queries.reshape(64, 8, QDIM), ("section", "yh", "z"))
        qb = swap(qa, 1)

    with jax.named_scope("attention"):
        place = jnp.stack([attn * span, (attn == 0).astype(jnp.int32)])
        keep, send = call(
            attend_kernel,
            [shaped(f32, 5, 512, 128), shaped(bf16, 512, PACK)],
            [SMEM, SMEM, VMEM, VMEM, HBM, VMEM],
            (
                lengths,
                place,
                qa.reshape(512, QDIM),
                qb.reshape(512, QDIM),
                jnp.swapaxes(cache, 1, 2),
                new_entry,
            ),
            [
                pltpu.VMEM((5, 1024, 128), f32),
                pltpu.VMEM((5, 512, 128), f32),
                pltpu.VMEM((8, QDIM, span), bf16),
                pltpu.SemaphoreType.DMA((8,)),
            ],
        )
        merged = call(merge_kernel, shaped(bf16, 512, PACK), [VMEM] * 2, (keep, swap(send, 1)))
        got = exchange(merged.reshape(64, 8, PACK), ("section", "yh", "z"))

    with jax.named_scope("output"):
        mid = call(
            combine_kernel,
            shaped(bf16, 16, ROWS, NOPE),
            [VMEM] * 2,
            (got.reshape(8, 64, PACK), first),
        )
        mids = exchange(mid, ("section", "yh"))
        outs = call(
            project_kernel,
            shaped(f32, ROWS, 512),
            [SMEM] + [VMEM] * 6,
            (where, mids, *pieces, others),
        )
        share = exchange(outs.reshape(8, 8, 512), ("z", "core"))
        mixed = call(total_kernel, shaped(bf16, 8, 448), [VMEM], (share,))
        return lax.ppermute(
            mixed,
            ALL,
            [
                (s * 16 + y * 8 + t, t * 16 + s * 2 + y)
                for s in range(8)
                for y in range(2)
                for t in range(8)
            ],
        )


def solution(mesh):
    split = Mesh(mesh.devices.reshape(8, 2, 4, 2), ALL)
    return jax.shard_map(
        on_device,
        mesh=split,
        in_specs=(
            P("section", None),
            P("section", ATTN),
            P("section", ATTN),
            P("section", ATTN),
            P("section", ATTN),
            P(None, ALL),
            P("section", ATTN, None),
            P("section", None),
            P("section"),
        ),
        out_specs=P("section", ATTN),
        check_vma=False,
    )
```
